32 devices in a mesh: tm: 8 (over z, y), cell: 4 (over x, core).
Axes of the slice: x: 2, y: 2, z: 4, core: 2. Of those that a mesh axis runs over, the one named last changes fastest.
Arguments:
- increments: int32 [768, 8192], P('cell', 'tm'), may hold values from 0 to 3
- noise: bfloat16 [768, 8192], P('cell', 'tm'), may hold values from -6 to 6
- noise_scale: float32 [768], P('cell'), may hold values from 0.5 to 4
- factor: bfloat16 [8192], replicated, may hold values from 0 to 2
Outputs:
- counts: int32 [768, 8192], P('cell', 'tm')
- correlated_noise: float32 [768, 8192], P('cell', 'tm')
- total_counts: int32 [8192], P('tm')
The draws below stay inside these ranges and needn't reach their ends.
All inputs are finite; a program needn't handle non-finite values.
Results may differ from the reference program's by a relative error of at most 0.0009.
Values may be sent and summed in bfloat16 or wider, within the bound.
A program may use at most 64 MiB of HBM per device.

```python
import math
import jax
import jax.numpy as jnp
from jax import lax

CELLS = 768
BLK = 512
TIME = 8192


def draw_factor(key, part):
    offsets = jnp.arange(TIME, dtype=jnp.float32)
    clamped = jnp.maximum(offsets, 1.0)
    inverse = 1.0 / clamped
    series = 1.0 - inverse / 8.0 + inverse ** 2 / 128.0 + 5.0 * inverse ** 3 / 1024.0 - 21.0 * inverse ** 4 / 32768.0
    far_value = series / jnp.sqrt(jnp.pi * clamped)
    step_range = jnp.arange(1, 32, dtype=jnp.float32)
    near_table = jnp.concatenate([jnp.ones((1,), jnp.float32), jnp.cumprod(1.0 - 0.5 / step_range)])
    near_value = near_table[jnp.minimum(jnp.arange(TIME, dtype=jnp.int32), 31)]
    baseline = jnp.where(offsets < 32.0, near_value, far_value)
    spread_key = jax.random.fold_in(key, 7)
    spread = jnp.exp(jax.random.uniform(spread_key, (TIME,), jnp.float32, math.log(0.5), math.log(2.0)))
    return (baseline * spread).astype(jnp.bfloat16)


def place_ends(result, own_key, low, largest):
    index_at = [jax.random.randint(jax.random.fold_in(own_key, axis), (), 0, length) for axis, length in enumerate(result.shape)]
    main_axis = result.shape.index(max(result.shape))
    neighbour = index_at[:main_axis] + [(index_at[main_axis] + 1) % result.shape[main_axis]] + index_at[main_axis + 1:]
    return result.at[tuple(index_at)].set(low).at[tuple(neighbour)].set(largest)


def block_scale(rng, shape, split, smallest, top_value):
    loudness = 1.0
    for axis_at, shards_of in split:
        draws = jax.random.uniform(jax.random.fold_in(jax.random.fold_in(rng, 6), axis_at), (shards_of,), jnp.float32, smallest / len(split), top_value / len(split))
        loudness = loudness * jnp.repeat(jnp.exp(draws), shape[axis_at] // shards_of).reshape((-1,) + (1,) * (len(shape) - 1 - axis_at))
    return loudness


def centred(key, extent, scale, bound, cuts=(), held_as=jnp.bfloat16):
    values = scale * jax.random.normal(key, extent, jnp.float32)
    if cuts:
        values = values * block_scale(key, extent, cuts, -0.22, 0.18)
    return jnp.clip(values, -bound, bound).astype(held_as)


def setup_inputs(seed: int = 0) -> dict:
    seeds = jax.random.split(jax.random.key(seed), 5)
    return {
        "increments": place_ends(jax.random.randint(seeds[0], (CELLS, TIME), 0, 4), jax.random.fold_in(seeds[0], 1), 0, 3).astype(jnp.int32),
        "noise": centred(seeds[1], (CELLS, TIME), 1.0, 6.0, ((0, 4), (1, 8))),
        "noise_scale": jnp.clip(jnp.exp(math.log(4.0) - 2.0794415 * jax.random.uniform(seeds[2], (CELLS,), jnp.float32) ** block_scale(seeds[2], (CELLS,), ((0, 4),), -0.2, 0.2)), 0.5, 4.0),
        "factor": draw_factor(jax.random.fold_in(seeds[4], 71), 0),
    }


def reference(increments, noise, noise_scale, factor):
    counts = jnp.cumsum(increments, axis=1, dtype=jnp.int32)
    total_counts = jnp.sum(counts, axis=0, dtype=jnp.int32)
    padded = jnp.concatenate([jnp.zeros((TIME,), jnp.float32), factor.astype(jnp.float32)])
    source = noise.astype(jnp.float32)
    pieces = []
    for target in range(TIME // BLK):
        last_col = (target + 1) * BLK
        source_ids = jnp.arange(last_col, dtype=jnp.int32)[:, None]
        target_ids = (target * BLK + jnp.arange(BLK, dtype=jnp.int32))[None, :]
        matrix = padded[(target_ids - source_ids + TIME).astype(jnp.int32)]
        pieces.append(jnp.dot(source[:, :last_col], matrix, precision=lax.Precision.HIGHEST, preferred_element_type=jnp.float32))
    convolved = jnp.concatenate(pieces, axis=1)
    correlated_noise = noise_scale[:, None] * convolved
    return counts, correlated_noise, total_counts
```

```python
import functools

import jax
import jax.numpy as jnp
from jax import lax
from jax.experimental import pallas as pl
from jax.experimental.pallas import tpu as pltpu
from jax.sharding import PartitionSpec as P

MESH = pl.DeviceIdType.MESH
DEPTH = 256
LANES = 128
WIDE = 512


def remote(src, dst, send_sem, recv_sem, target):
    return pltpu.make_async_remote_copy(
        src_ref=src,
        dst_ref=dst,
        send_sem=send_sem,
        recv_sem=recv_sem,
        device_id=target,
        device_id_type=MESH,
    )


def kernel(
    n, m, inc_ref, noise_ref, fac_ref, counts_ref, conv_ref, total_ref,
    held, near, strip, acc, give, got, sums, steps, incb,
    up_send, up_recv, pair_send, pair_recv, sum_send, sum_recv, step_send, step_recv,
):
    rows, seg = noise_ref.shape
    half = rows // 2
    pair = 2 * seg
    me = lax.axis_index("tm")
    cell = lax.axis_index("cell")
    level, side = me // 2, me % 2
    mate = me + 1 - 2 * side
    levels = n // 2

    barrier = pltpu.get_barrier_semaphore()
    for i in range(1, n):
        pl.semaphore_signal(barrier, inc=1, device_id={"tm": lax.rem(me + i, n)}, device_id_type=MESH)
    for i in range(1, m):
        pl.semaphore_signal(barrier, inc=1, device_id={"cell": lax.rem(cell + i, m)}, device_id_type=MESH)
    pl.semaphore_wait(barrier, n + m - 2)

    mine = pl.ds(pl.multiple_of(side * half, 16), half)
    theirs = pl.ds(pl.multiple_of((1 - side) * half, 16), half)

    def lift(q):
        return remote(held.at[q], held.at[q], up_send.at[q], up_recv.at[q], {"tm": jnp.minimum(me + 2, n - 2 + side)})

    def raise_(q):
        @pl.when(level < levels - 1)
        def _():
            lift(q).start()

    swap = remote(noise_ref.at[theirs], held.at[me], pair_send.at[0], pair_recv.at[0], {"tm": mate})
    swap.start()
    rest = remote(noise_ref.at[mine], near, pair_send.at[2], pair_recv.at[2], {"tm": mate})

    @pl.when(side == 0)
    def _():
        rest.start()

    held[me] = noise_ref[mine]
    raise_(me)

    incb[...] = inc_ref[...].astype(jnp.float32).astype(jnp.bfloat16)
    sums[me] = jnp.zeros(sums.shape[1:], jnp.float32)
    sums[me, :, :rows] = lax.dot_general(
        jnp.ones((8, seg), jnp.bfloat16), incb[...], (((1,), (1,)), ((), ())),
        preferred_element_type=jnp.float32,
    )

    def tell(i):
        return remote(sums.at[me], sums.at[me], sum_send.at[i], sum_recv.at[me], {"tm": lax.rem(me + i, n)})

    def heard(i):
        other = lax.rem(me + i, n)
        return remote(sums.at[other], sums.at[other], sum_send.at[i], sum_recv.at[other], {"tm": other})

    for i in range(1, n):
        tell(i).start()

    strip[LANES:, :LANES] = jnp.zeros((LANES, LANES), jnp.bfloat16)

    def lay(chunk):
        at = pl.multiple_of(chunk * seg, LANES)
        slab = fac_ref[:, pl.ds(pl.multiple_of(chunk * seg, LANES), seg + LANES)]
        spread = jnp.broadcast_to(slab, (LANES, seg + LANES))
        skew = pltpu.roll(spread, 0, 1, stride=1, stride_axis=0)[:, LANES:].astype(jnp.bfloat16)
        strip[:LANES, pl.ds(at, seg)] = skew
        strip[LANES:, pl.ds(at + LANES, seg)] = skew

    def convolve(q):
        def part(w, carry):
            cols = pl.ds(pl.multiple_of(w * WIDE, LANES), WIDE)
            total = acc[:, cols]
            for k in range(seg // DEPTH):
                lag = pair * level - seg * q - DEPTH * k
                taps = strip[:, pl.ds(pl.multiple_of(lag + w * WIDE, LANES), WIDE)]
                total += jnp.dot(
                    held[q, :, k * DEPTH : (k + 1) * DEPTH], taps, preferred_element_type=jnp.float32
                )
            acc[:, cols] = total
            return carry

        lax.fori_loop(0, pair // WIDE, part, 0)

    lay(0)
    lay(1)
    acc[...] = jnp.zeros_like(acc)
    conv_ref[...] = jnp.dot(noise_ref[:, :DEPTH], strip[:, :seg], preferred_element_type=jnp.float32)
    for k in range(1, seg // DEPTH):
        conv_ref[:, k * DEPTH :] += jnp.dot(
            noise_ref[:, k * DEPTH : (k + 1) * DEPTH], strip[:, : seg - k * DEPTH], preferred_element_type=jnp.float32
        )
    swap.wait_recv()
    raise_(mate)

    @pl.when(side == 1)
    def _():
        rest.wait_recv()
        for where, block in ((theirs, near), (mine, held.at[mate])):
            total = conv_ref[where]
            for k in range(seg // DEPTH):
                taps = strip[:, seg - k * DEPTH : 2 * seg - k * DEPTH]
                total += jnp.dot(block[:, k * DEPTH : (k + 1) * DEPTH], taps, preferred_element_type=jnp.float32)
            conv_ref[where] = total

    for i in range(1, n):
        heard(i).wait_recv()
    before = jnp.zeros(sums.shape[1:], jnp.float32)
    for q in range(n):
        before += jnp.where(q < me, sums[q], 0.0)
    wide = sums.shape[2]
    diag = lax.broadcasted_iota(jnp.int32, (rows, wide), 0) == lax.broadcasted_iota(jnp.int32, (rows, wide), 1)
    carry = jnp.sum(jnp.where(diag, jnp.broadcast_to(before[0:1], (rows, wide)), 0.0), axis=1, keepdims=True)
    ones = (
        lax.broadcasted_iota(jnp.int32, (DEPTH, DEPTH), 0) <= lax.broadcasted_iota(jnp.int32, (DEPTH, DEPTH), 1)
    ).astype(jnp.float32).astype(jnp.bfloat16)
    for k in range(seg // DEPTH):
        cols = slice(k * DEPTH, (k + 1) * DEPTH)
        run = jnp.dot(incb[:, cols], ones, preferred_element_type=jnp.float32) + carry
        counts_ref[:, cols] = run.astype(jnp.int32)
        steps[cell, :, cols] = jnp.broadcast_to(jnp.sum(run, axis=0, keepdims=True).astype(jnp.int32), (8, DEPTH))
        carry = run[:, DEPTH - 1 :]

    def show(i):
        return remote(steps.at[cell], steps.at[cell], step_send.at[i], step_recv.at[cell], {"cell": lax.rem(cell + i, m)})

    def seen(i):
        other = lax.rem(cell + i, m)
        return remote(steps.at[other], steps.at[other], step_send.at[i], step_recv.at[other], {"cell": other})

    for i in range(1, m):
        show(i).start()

    def step(j, carry):
        lay(2 * j)
        lay(2 * j + 1)
        for q in (2 * (level - j) + side, 2 * (level - j) + 1 - side):
            lift(q).wait_recv()
            raise_(q)
            convolve(q)
        return carry

    lax.fori_loop(1, level + 1, step, 0)

    back = remote(give, got, pair_send.at[1], pair_recv.at[1], {"tm": mate})

    @pl.when(level > 0)
    def _():
        give[...] = acc[:, pl.ds(pl.multiple_of((1 - side) * seg, LANES), seg)].astype(jnp.bfloat16)
        back.start()
        conv_ref[mine] += acc[:, pl.ds(pl.multiple_of(side * seg, LANES), seg)]

    for i in range(1, m):
        seen(i).wait_recv()
    all_steps = steps[0, 0:1]
    for c in range(1, m):
        all_steps += steps[c, 0:1]
    total_ref[...] = all_steps

    @pl.when(level > 0)
    def _():
        back.wait_recv()
        conv_ref[theirs] += got[...].astype(jnp.float32)
        back.wait_send()

    @pl.when(side == 0)
    def _():
        rest.wait_send()

    swap.wait_send()
    for i in range(1, n):
        tell(i).wait_send()
    for i in range(1, m):
        show(i).wait_send()

    @pl.when(level < levels - 1)
    def _():
        def left(q, carry):
            lift(q).wait_send()
            return carry

        lax.fori_loop(0, 2 * level + 2, left, 0)


def solution(mesh):
    n, m = mesh.shape["tm"], mesh.shape["cell"]

    def shards(increments, noise, noise_scale, factor):
        rows, seg = noise.shape
        half = rows // 2
        wide = -(-rows // LANES) * LANES
        fac = jnp.pad(factor.astype(jnp.float32), (LANES, 0))[None, :]
        vmem = pl.BlockSpec(memory_space=pltpu.VMEM)
        dma = pltpu.SemaphoreType.DMA
        counts, conv, total = pl.pallas_call(
            functools.partial(kernel, n, m),
            out_shape=(
                jax.ShapeDtypeStruct((rows, seg), jnp.int32),
                jax.ShapeDtypeStruct((rows, seg), jnp.float32),
                jax.ShapeDtypeStruct((1, seg), jnp.int32),
            ),
            in_specs=[vmem] * 3,
            out_specs=(vmem,) * 3,
            scratch_shapes=[
                pltpu.VMEM((n, half, seg), jnp.bfloat16),
                pltpu.VMEM((half, seg), jnp.bfloat16),
                pltpu.VMEM((DEPTH, n * seg + LANES), jnp.bfloat16),
                pltpu.VMEM((half, 2 * seg), jnp.float32),
                pltpu.VMEM((half, seg), jnp.bfloat16),
                pltpu.VMEM((half, seg), jnp.bfloat16),
                pltpu.VMEM((n, 8, wide), jnp.float32),
                pltpu.VMEM((m, 8, seg), jnp.int32),
                pltpu.VMEM((rows, seg), jnp.bfloat16),
                dma((n,)), dma((n,)), dma((3,)), dma((3,)), dma((n,)), dma((n,)), dma((m,)), dma((m,)),
            ],
            compiler_params=pltpu.CompilerParams(
                collective_id=0, has_side_effects=True, vmem_limit_bytes=50 * 2**20
            ),
        )(increments, noise, fac)
        return counts, noise_scale[:, None] * conv, total[0]

    return jax.shard_map(
        shards,
        mesh=mesh,
        in_specs=(P("cell", "tm"), P("cell", "tm"), P("cell"), P()),
        out_specs=(P("cell", "tm"), P("cell", "tm"), P("tm")),
        check_vma=False,
    )
```

```python
import functools

import jax
import jax.numpy as jnp
from jax import lax
from jax.experimental import pallas as pl
from jax.experimental.pallas import tpu as pltpu
from jax.sharding import PartitionSpec as P

MESH = pl.DeviceIdType.MESH
DEPTH = 256
LANES = 128
WIDE = 512


def remote(src, dst, send_sem, recv_sem, target):
    return pltpu.make_async_remote_copy(
        src_ref=src,
        dst_ref=dst,
        send_sem=send_sem,
        recv_sem=recv_sem,
        device_id=target,
        device_id_type=MESH,
    )


def kernel(
    n, m, inc_hbm, noise_hbm, scale_ref, fac_ref, counts_ref, conv_ref, total_ref,
    inc_ref, noise_ref, fetch, held, near, strip, acc, give, got, sums, steps, incb, gains,
    up_send, up_recv, pair_send, pair_recv, sum_send, sum_recv, step_send, step_recv,
):
    rows, seg = noise_hbm.shape
    half = rows // 2
    pair = 2 * seg
    me = lax.axis_index("tm")
    cell = lax.axis_index("cell")
    level, side = me // 2, me % 2
    mate = me + 1 - 2 * side
    levels = n // 2

    noise_in = pltpu.make_async_copy(noise_hbm, noise_ref, fetch.at[0])
    inc_in = pltpu.make_async_copy(inc_hbm, inc_ref, fetch.at[1])
    noise_in.start()
    inc_in.start()
    barrier = pltpu.get_barrier_semaphore()
    for i in range(1, n):
        pl.semaphore_signal(barrier, inc=1, device_id={"tm": lax.rem(me + i, n)}, device_id_type=MESH)
    for i in range(1, m):
        pl.semaphore_signal(barrier, inc=1, device_id={"cell": lax.rem(cell + i, m)}, device_id_type=MESH)
    wide = sums.shape[2]
    diag = lax.broadcasted_iota(jnp.int32, (rows, wide), 0) == lax.broadcasted_iota(jnp.int32, (rows, wide), 1)

    def column(row):
        return jnp.sum(jnp.where(diag, jnp.broadcast_to(row, (rows, wide)), 0.0), axis=1, keepdims=True)

    noise_in.wait()
    pl.semaphore_wait(barrier, n + m - 2)

    mine = pl.ds(pl.multiple_of(side * half, 16), half)
    theirs = pl.ds(pl.multiple_of((1 - side) * half, 16), half)

    def lift(q):
        return remote(held.at[q], held.at[q], up_send.at[q], up_recv.at[q], {"tm": jnp.minimum(me + 2, n - 2 + side)})

    def raise_(q):
        @pl.when(level < levels - 1)
        def _():
            lift(q).start()

    swap = remote(noise_ref.at[theirs], held.at[me], pair_send.at[0], pair_recv.at[0], {"tm": mate})
    swap.start()
    rest = remote(noise_ref.at[mine], near, pair_send.at[2], pair_recv.at[2], {"tm": mate})
    held[me] = noise_ref[mine]
    raise_(me)
    inc_in.wait()

    incb[...] = inc_ref[...].astype(jnp.float32).astype(jnp.bfloat16)
    sums[me] = jnp.zeros(sums.shape[1:], jnp.float32)
    sums[me, :, :rows] = lax.dot_general(
        jnp.ones((8, seg), jnp.bfloat16), incb[...], (((1,), (1,)), ((), ())),
        preferred_element_type=jnp.float32,
    )

    def tell(i):
        return remote(sums.at[me], sums.at[me], sum_send.at[i], sum_recv.at[me], {"tm": lax.rem(me + i, n)})

    def heard(i):
        other = lax.rem(me + i, n)
        return remote(sums.at[other], sums.at[other], sum_send.at[i], sum_recv.at[other], {"tm": other})

    for i in range(1, n):
        tell(i).start()

    @pl.when(side == 0)
    def _():
        rest.start()

    strip[LANES:, :LANES] = jnp.zeros((LANES, LANES), jnp.bfloat16)

    def lay(chunk):
        at = pl.multiple_of(chunk * seg, LANES)
        slab = fac_ref[:, pl.ds(pl.multiple_of(chunk * seg, LANES), seg + LANES)]
        spread = jnp.broadcast_to(slab, (LANES, seg + LANES))
        skew = pltpu.roll(spread, 0, 1, stride=1, stride_axis=0)[:, LANES:].astype(jnp.bfloat16)
        strip[:LANES, pl.ds(at, seg)] = skew
        strip[LANES:, pl.ds(at + LANES, seg)] = skew

    def convolve(q):
        def part(w, carry):
            cols = pl.ds(pl.multiple_of(w * WIDE, LANES), WIDE)
            total = acc[:, cols]
            for k in range(seg // DEPTH):
                lag = pair * level - seg * q - DEPTH * k
                taps = strip[:, pl.ds(pl.multiple_of(lag + w * WIDE, LANES), WIDE)]
                total += jnp.dot(
                    held[q, :, k * DEPTH : (k + 1) * DEPTH], taps, preferred_element_type=jnp.float32
                )
            acc[:, cols] = total
            return carry

        lax.fori_loop(0, pair // WIDE, part, 0)

    lay(0)
    lay(1)
    acc[...] = jnp.zeros_like(acc)
    conv_ref[...] = jnp.dot(noise_ref[:, :DEPTH], strip[:, :seg], preferred_element_type=jnp.float32)
    for k in range(1, seg // DEPTH):
        conv_ref[:, k * DEPTH :] += jnp.dot(
            noise_ref[:, k * DEPTH : (k + 1) * DEPTH], strip[:, : seg - k * DEPTH], preferred_element_type=jnp.float32
        )
    swap.wait_recv()
    raise_(mate)

    @pl.when(side == 1)
    def _():
        rest.wait_recv()
        for where, block in ((theirs, near), (mine, held.at[mate])):
            total = conv_ref[where]
            for k in range(seg // DEPTH):
                taps = strip[:, seg - k * DEPTH : 2 * seg - k * DEPTH]
                total += jnp.dot(block[:, k * DEPTH : (k + 1) * DEPTH], taps, preferred_element_type=jnp.float32)
            conv_ref[where] = total

    for i in range(1, n):
        heard(i).wait_recv()
    before = jnp.zeros(sums.shape[1:], jnp.float32)
    for q in range(n):
        before += jnp.where(q < me, sums[q], 0.0)
    carry = column(before[0:1])
    ones = (
        lax.broadcasted_iota(jnp.int32, (DEPTH, DEPTH), 0) <= lax.broadcasted_iota(jnp.int32, (DEPTH, DEPTH), 1)
    ).astype(jnp.float32).astype(jnp.bfloat16)
    for k in range(seg // DEPTH):
        cols = slice(k * DEPTH, (k + 1) * DEPTH)
        run = jnp.dot(incb[:, cols], ones, preferred_element_type=jnp.float32) + carry
        counts_ref[:, cols] = run.astype(jnp.int32)
        steps[cell, :, cols] = jnp.broadcast_to(jnp.sum(run, axis=0, keepdims=True).astype(jnp.int32), (8, DEPTH))
        carry = run[:, DEPTH - 1 :]

    def show(i):
        return remote(steps.at[cell], steps.at[cell], step_send.at[i], step_recv.at[cell], {"cell": lax.rem(cell + i, m)})

    def seen(i):
        other = lax.rem(cell + i, m)
        return remote(steps.at[other], steps.at[other], step_send.at[i], step_recv.at[other], {"cell": other})

    for i in range(1, m):
        show(i).start()

    def step(j, carry):
        lay(2 * j)
        lay(2 * j + 1)
        for q in (2 * (level - j) + side, 2 * (level - j) + 1 - side):
            lift(q).wait_recv()
            raise_(q)
            convolve(q)
        return carry

    lax.fori_loop(1, level + 1, step, 0)

    gain = column(scale_ref[...])
    gains[...] = jnp.broadcast_to(gain, gains.shape)
    back = remote(give, got, pair_send.at[1], pair_recv.at[1], {"tm": mate})

    @pl.when(level > 0)
    def _():
        give[...] = acc[:, pl.ds(pl.multiple_of((1 - side) * seg, LANES), seg)].astype(jnp.bfloat16)
        back.start()
        conv_ref[mine] = (conv_ref[mine] + acc[:, pl.ds(pl.multiple_of(side * seg, LANES), seg)]) * gains[mine, 0:1]

    @pl.when(level == 0)
    def _():
        conv_ref[...] = conv_ref[...] * gains[:, 0:1]

    for i in range(1, m):
        seen(i).wait_recv()
    all_steps = steps[0, 0:1]
    for c in range(1, m):
        all_steps += steps[c, 0:1]
    total_ref[...] = all_steps

    @pl.when(level > 0)
    def _():
        back.wait_recv()
        conv_ref[theirs] = (conv_ref[theirs] + got[...].astype(jnp.float32)) * gains[theirs, 0:1]
        back.wait_send()

    @pl.when(side == 0)
    def _():
        rest.wait_send()

    swap.wait_send()
    for i in range(1, n):
        tell(i).wait_send()
    for i in range(1, m):
        show(i).wait_send()

    @pl.when(level < levels - 1)
    def _():
        def left(q, carry):
            lift(q).wait_send()
            return carry

        lax.fori_loop(0, 2 * level + 2, left, 0)


def solution(mesh):
    n, m = mesh.shape["tm"], mesh.shape["cell"]

    def shards(increments, noise, noise_scale, factor):
        rows, seg = noise.shape
        half = rows // 2
        wide = -(-rows // LANES) * LANES
        fac = jnp.pad(factor.astype(jnp.float32), (LANES, 0))[None, :]
        hbm = pl.BlockSpec(memory_space=pltpu.HBM)
        gain = jnp.pad(noise_scale, (0, wide - rows))[None, :]
        vmem = pl.BlockSpec(memory_space=pltpu.VMEM)
        dma = pltpu.SemaphoreType.DMA
        counts, conv, total = pl.pallas_call(
            functools.partial(kernel, n, m),
            out_shape=(
                jax.ShapeDtypeStruct((rows, seg), jnp.int32),
                jax.ShapeDtypeStruct((rows, seg), jnp.float32),
                jax.ShapeDtypeStruct((1, seg), jnp.int32),
            ),
            in_specs=[hbm, hbm, vmem, vmem],
            out_specs=(vmem,) * 3,
            scratch_shapes=[
                pltpu.VMEM((rows, seg), jnp.int32),
                pltpu.VMEM((rows, seg), jnp.bfloat16),
                dma((2,)),
                pltpu.VMEM((n, half, seg), jnp.bfloat16),
                pltpu.VMEM((half, seg), jnp.bfloat16),
                pltpu.VMEM((DEPTH, n * seg + LANES), jnp.bfloat16),
                pltpu.VMEM((half, 2 * seg), jnp.float32),
                pltpu.VMEM((half, seg), jnp.bfloat16),
                pltpu.VMEM((half, seg), jnp.bfloat16),
                pltpu.VMEM((n, 8, wide), jnp.float32),
                pltpu.VMEM((m, 8, seg), jnp.int32),
                pltpu.VMEM((rows, seg), jnp.bfloat16),
                pltpu.VMEM((rows, LANES), jnp.float32),
                dma((n,)), dma((n,)), dma((3,)), dma((3,)), dma((n,)), dma((n,)), dma((m,)), dma((m,)),
            ],
            compiler_params=pltpu.CompilerParams(
                collective_id=0, has_side_effects=True, vmem_limit_bytes=50 * 2**20
            ),
        )(increments, noise, gain, fac)
        return counts, conv, total[0]

    return jax.shard_map(
        shards,
        mesh=mesh,
        in_specs=(P("cell", "tm"), P("cell", "tm"), P("cell"), P()),
        out_specs=(P("cell", "tm"), P("cell", "tm"), P("tm")),
        check_vma=False,
    )
```

```python
import functools

import jax
import jax.numpy as jnp
from jax import lax
from jax.experimental import pallas as pl
from jax.experimental.pallas import tpu as pltpu
from jax.sharding import PartitionSpec as P

MESH = pl.DeviceIdType.MESH
DEPTH = 256
LANES = 128
WIDE = 512


def remote(src, dst, send_sem, recv_sem, target):
    return pltpu.make_async_remote_copy(
        src_ref=src,
        dst_ref=dst,
        send_sem=send_sem,
        recv_sem=recv_sem,
        device_id=target,
        device_id_type=MESH,
    )


def kernel(
    n, m, inc_hbm, noise_hbm, scale_ref, fac_ref, counts_ref, conv_ref, total_ref,
    inc_ref, noise_ref, fetch, held, near, strip, acc, give, got, sums, steps, incb, gains,
    up_send, up_recv, pair_send, pair_recv, sum_send, sum_recv, step_send, step_recv,
):
    rows, seg = noise_hbm.shape
    half = rows // 2
    pair = 2 * seg
    me = lax.axis_index("tm")
    cell = lax.axis_index("cell")
    level, side = me // 2, me % 2
    mate = me + 1 - 2 * side
    levels = n // 2

    noise_in = pltpu.make_async_copy(noise_hbm, noise_ref, fetch.at[0])
    inc_in = pltpu.make_async_copy(inc_hbm, inc_ref, fetch.at[1])
    noise_in.start()
    inc_in.start()
    barrier = pltpu.get_barrier_semaphore()
    for i in range(1, n):
        pl.semaphore_signal(barrier, inc=1, device_id={"tm": lax.rem(me + i, n)}, device_id_type=MESH)
    for i in range(1, m):
        pl.semaphore_signal(barrier, inc=1, device_id={"cell": lax.rem(cell + i, m)}, device_id_type=MESH)
    wide = sums.shape[2]
    diag = lax.broadcasted_iota(jnp.int32, (rows, wide), 0) == lax.broadcasted_iota(jnp.int32, (rows, wide), 1)

    def column(row):
        return jnp.sum(jnp.where(diag, jnp.broadcast_to(row, (rows, wide)), 0.0), axis=1, keepdims=True)

    noise_in.wait()
    pl.semaphore_wait(barrier, n + m - 2)

    mine = pl.ds(pl.multiple_of(side * half, 16), half)
    theirs = pl.ds(pl.multiple_of((1 - side) * half, 16), half)

    def lift(q):
        return remote(held.at[q], held.at[q], up_send.at[q], up_recv.at[q], {"tm": jnp.minimum(me + 2, n - 2 + side)})

    def raise_(q):
        @pl.when(level < levels - 1)
        def _():
            lift(q).start()

    swap = remote(noise_ref.at[theirs], held.at[me], pair_send.at[0], pair_recv.at[0], {"tm": mate})
    swap.start()
    rest = remote(noise_ref.at[mine], near, pair_send.at[2], pair_recv.at[2], {"tm": mate})
    held[me] = noise_ref[mine]
    raise_(me)
    inc_in.wait()

    incb[...] = inc_ref[...].astype(jnp.float32).astype(jnp.bfloat16)
    sums[me] = jnp.zeros(sums.shape[1:], jnp.float32)
    sums[me, :, :rows] = lax.dot_general(
        jnp.ones((8, seg), jnp.bfloat16), incb[...], (((1,), (1,)), ((), ())),
        preferred_element_type=jnp.float32,
    )

    def tell(i):
        return remote(sums.at[me], sums.at[me], sum_send.at[i], sum_recv.at[me], {"tm": lax.rem(me + i, n)})

    def heard(i):
        other = lax.rem(me + i, n)
        return remote(sums.at[other], sums.at[other], sum_send.at[i], sum_recv.at[other], {"tm": other})

    for i in range(1, n):
        tell(i).start()

    @pl.when(side == 0)
    def _():
        rest.start()

    strip[LANES:, :LANES] = jnp.zeros((LANES, LANES), jnp.bfloat16)

    def lay(chunk):
        at = pl.multiple_of(chunk * seg, LANES)
        slab = fac_ref[:, pl.ds(pl.multiple_of(chunk * seg, LANES), seg + LANES)]
        spread = jnp.broadcast_to(slab, (LANES, seg + LANES))
        skew = pltpu.roll(spread, 0, 1, stride=1, stride_axis=0)[:, LANES:].astype(jnp.bfloat16)
        strip[:LANES, pl.ds(at, seg)] = skew
        strip[LANES:, pl.ds(at + LANES, seg)] = skew

    def convolve(q):
        def part(w, carry):
            cols = pl.ds(pl.multiple_of(w * WIDE, LANES), WIDE)
            total = acc[:, cols]
            for k in range(seg // DEPTH):
                lag = pair * level - seg * q - DEPTH * k
                taps = strip[:, pl.ds(pl.multiple_of(lag + w * WIDE, LANES), WIDE)]
                total += jnp.dot(
                    held[q, :, k * DEPTH : (k + 1) * DEPTH], taps, preferred_element_type=jnp.float32
                )
            acc[:, cols] = total
            return carry

        lax.fori_loop(0, pair // WIDE, part, 0)

    first = 2 * (level - 1) + side
    acc[...] = jnp.zeros_like(acc)
    swap.wait_recv()
    raise_(mate)

    @pl.when(level > 0)
    def _():
        lift(first).wait_recv()
        raise_(first)

    lay(0)
    lay(1)
    conv_ref[...] = jnp.dot(noise_ref[:, :DEPTH], strip[:, :seg], preferred_element_type=jnp.float32)
    for k in range(1, seg // DEPTH):
        conv_ref[:, k * DEPTH :] += jnp.dot(
            noise_ref[:, k * DEPTH : (k + 1) * DEPTH], strip[:, : seg - k * DEPTH], preferred_element_type=jnp.float32
        )

    @pl.when(side == 1)
    def _():
        rest.wait_recv()
        for where, block in ((theirs, near), (mine, held.at[mate])):
            total = conv_ref[where]
            for k in range(seg // DEPTH):
                taps = strip[:, seg - k * DEPTH : 2 * seg - k * DEPTH]
                total += jnp.dot(block[:, k * DEPTH : (k + 1) * DEPTH], taps, preferred_element_type=jnp.float32)
            conv_ref[where] = total

    def step(j, carry):
        lay(2 * j)
        lay(2 * j + 1)
        for q in (2 * (level - j) + side, 2 * (level - j) + 1 - side):

            @pl.when(q != first)
            def _():
                lift(q).wait_recv()
                raise_(q)

            convolve(q)
        return carry

    lax.fori_loop(1, level + 1, step, 0)

    gain = column(scale_ref[...])
    gains[...] = jnp.broadcast_to(gain, gains.shape)
    back = remote(give, got, pair_send.at[1], pair_recv.at[1], {"tm": mate})

    @pl.when(level > 0)
    def _():
        give[...] = acc[:, pl.ds(pl.multiple_of((1 - side) * seg, LANES), seg)].astype(jnp.bfloat16)
        back.start()
        conv_ref[mine] = (conv_ref[mine] + acc[:, pl.ds(pl.multiple_of(side * seg, LANES), seg)]) * gains[mine, 0:1]

    @pl.when(level == 0)
    def _():
        conv_ref[...] = conv_ref[...] * gains[:, 0:1]

    for i in range(1, n):
        heard(i).wait_recv()
    before = jnp.zeros(sums.shape[1:], jnp.float32)
    for q in range(n):
        before += jnp.where(q < me, sums[q], 0.0)
    carry = column(before[0:1])
    ones = (
        lax.broadcasted_iota(jnp.int32, (DEPTH, DEPTH), 0) <= lax.broadcasted_iota(jnp.int32, (DEPTH, DEPTH), 1)
    ).astype(jnp.float32).astype(jnp.bfloat16)
    for k in range(seg // DEPTH):
        cols = slice(k * DEPTH, (k + 1) * DEPTH)
        run = jnp.dot(incb[:, cols], ones, preferred_element_type=jnp.float32) + carry
        counts_ref[:, cols] = run.astype(jnp.int32)
        steps[cell, :, cols] = jnp.broadcast_to(jnp.sum(run, axis=0, keepdims=True).astype(jnp.int32), (8, DEPTH))
        carry = run[:, DEPTH - 1 :]

    def show(i):
        return remote(steps.at[cell], steps.at[cell], step_send.at[i], step_recv.at[cell], {"cell": lax.rem(cell + i, m)})

    def seen(i):
        other = lax.rem(cell + i, m)
        return remote(steps.at[other], steps.at[other], step_send.at[i], step_recv.at[other], {"cell": other})

    for i in range(1, m):
        show(i).start()

    for i in range(1, m):
        seen(i).wait_recv()
    all_steps = steps[0, 0:1]
    for c in range(1, m):
        all_steps += steps[c, 0:1]
    total_ref[...] = all_steps

    @pl.when(level > 0)
    def _():
        back.wait_recv()
        conv_ref[theirs] = (conv_ref[theirs] + got[...].astype(jnp.float32)) * gains[theirs, 0:1]
        back.wait_send()

    @pl.when(side == 0)
    def _():
        rest.wait_send()

    swap.wait_send()
    for i in range(1, n):
        tell(i).wait_send()
    for i in range(1, m):
        show(i).wait_send()

    @pl.when(level < levels - 1)
    def _():
        def left(q, carry):
            lift(q).wait_send()
            return carry

        lax.fori_loop(0, 2 * level + 2, left, 0)


def solution(mesh):
    n, m = mesh.shape["tm"], mesh.shape["cell"]

    def shards(increments, noise, noise_scale, factor):
        rows, seg = noise.shape
        half = rows // 2
        wide = -(-rows // LANES) * LANES
        fac = jnp.pad(factor.astype(jnp.float32), (LANES, 0))[None, :]
        hbm = pl.BlockSpec(memory_space=pltpu.HBM)
        gain = jnp.pad(noise_scale, (0, wide - rows))[None, :]
        vmem = pl.BlockSpec(memory_space=pltpu.VMEM)
        dma = pltpu.SemaphoreType.DMA
        counts, conv, total = pl.pallas_call(
            functools.partial(kernel, n, m),
            out_shape=(
                jax.ShapeDtypeStruct((rows, seg), jnp.int32),
                jax.ShapeDtypeStruct((rows, seg), jnp.float32),
                jax.ShapeDtypeStruct((1, seg), jnp.int32),
            ),
            in_specs=[hbm, hbm, vmem, vmem],
            out_specs=(vmem,) * 3,
            scratch_shapes=[
                pltpu.VMEM((rows, seg), jnp.int32),
                pltpu.VMEM((rows, seg), jnp.bfloat16),
                dma((2,)),
                pltpu.VMEM((n, half, seg), jnp.bfloat16),
                pltpu.VMEM((half, seg), jnp.bfloat16),
                pltpu.VMEM((DEPTH, n * seg + LANES), jnp.bfloat16),
                pltpu.VMEM((half, 2 * seg), jnp.float32),
                pltpu.VMEM((half, seg), jnp.bfloat16),
                pltpu.VMEM((half, seg), jnp.bfloat16),
                pltpu.VMEM((n, 8, wide), jnp.float32),
                pltpu.VMEM((m, 8, seg), jnp.int32),
                pltpu.VMEM((rows, seg), jnp.bfloat16),
                pltpu.VMEM((rows, LANES), jnp.float32),
                dma((n,)), dma((n,)), dma((3,)), dma((3,)), dma((n,)), dma((n,)), dma((m,)), dma((m,)),
            ],
            compiler_params=pltpu.CompilerParams(
                collective_id=0, has_side_effects=True, vmem_limit_bytes=52 * 2**20
            ),
        )(increments, noise, gain, fac)
        return counts, conv, total[0]

    return jax.shard_map(
        shards,
        mesh=mesh,
        in_specs=(P("cell", "tm"), P("cell", "tm"), P("cell"), P()),
        out_specs=(P("cell", "tm"), P("cell", "tm"), P("tm")),
        check_vma=False,
    )
```

```python
import functools

import jax
import jax.numpy as jnp
from jax import lax
from jax.experimental import pallas as pl
from jax.experimental.pallas import tpu as pltpu
from jax.sharding import PartitionSpec as P

MESH = pl.DeviceIdType.MESH
DEPTH = 256
LANES = 128
WIDE = 512


def remote(src, dst, send_sem, recv_sem, target):
    return pltpu.make_async_remote_copy(
        src_ref=src,
        dst_ref=dst,
        send_sem=send_sem,
        recv_sem=recv_sem,
        device_id=target,
        device_id_type=MESH,
    )


def kernel(
    n, m, inc_hbm, noise_hbm, scale_ref, fac_ref, counts_ref, conv_ref, total_ref,
    inc_ref, noise_ref, fetch, held, near, strip, acc, give, got, sums, steps, incb, gains,
    up_send, up_recv, pair_send, pair_recv, sum_send, sum_recv, step_send, step_recv,
):
    rows, seg = noise_hbm.shape
    half = rows // 2
    pair = 2 * seg
    me = lax.axis_index("tm")
    cell = lax.axis_index("cell")
    level, side = me // 2, me % 2
    mate = me + 1 - 2 * side
    levels = n // 2

    noise_in = pltpu.make_async_copy(noise_hbm, noise_ref, fetch.at[0])
    inc_in = pltpu.make_async_copy(inc_hbm, inc_ref, fetch.at[1])
    noise_in.start()
    inc_in.start()
    barrier = pltpu.get_barrier_semaphore()
    for i in range(1, n):
        pl.semaphore_signal(barrier, inc=1, device_id={"tm": lax.rem(me + i, n)}, device_id_type=MESH)
    for i in range(1, m):
        pl.semaphore_signal(barrier, inc=1, device_id={"cell": lax.rem(cell + i, m)}, device_id_type=MESH)
    diag = lax.broadcasted_iota(jnp.int32, (rows, rows), 0) == lax.broadcasted_iota(jnp.int32, (rows, rows), 1)

    def column(row):
        return jnp.sum(jnp.where(diag, jnp.broadcast_to(row, (rows, rows)), 0.0), axis=1, keepdims=True)

    noise_in.wait()
    pl.semaphore_wait(barrier, n + m - 2)

    mine = pl.ds(pl.multiple_of(side * half, 16), half)
    theirs = pl.ds(pl.multiple_of((1 - side) * half, 16), half)

    def lift(q):
        return remote(held.at[q], held.at[q], up_send.at[q], up_recv.at[q], {"tm": jnp.minimum(me + 2, n - 2 + side)})

    def raise_(q):
        @pl.when(level < levels - 1)
        def _():
            lift(q).start()

    swap = remote(noise_ref.at[theirs], held.at[me], pair_send.at[0], pair_recv.at[0], {"tm": mate})
    swap.start()
    rest = remote(noise_ref.at[mine], near, pair_send.at[2], pair_recv.at[2], {"tm": mate})
    held[me] = noise_ref[mine]
    raise_(me)
    inc_in.wait()

    incb[...] = inc_ref[...].astype(jnp.float32).astype(jnp.bfloat16)
    sums[me] = jnp.zeros(sums.shape[1:], jnp.float32)
    sums[me, :, :rows] = lax.dot_general(
        jnp.ones((8, seg), jnp.bfloat16), incb[...], (((1,), (1,)), ((), ())),
        preferred_element_type=jnp.float32,
    )

    def tell(i):
        return remote(sums.at[me], sums.at[me], sum_send.at[i], sum_recv.at[me], {"tm": lax.rem(me + i, n)})

    def heard(i):
        other = lax.rem(me + i, n)
        return remote(sums.at[other], sums.at[other], sum_send.at[i], sum_recv.at[other], {"tm": other})

    for i in range(1, n):
        tell(i).start()

    @pl.when(side == 0)
    def _():
        rest.start()

    strip[LANES:, :LANES] = jnp.zeros((LANES, LANES), jnp.bfloat16)

    def lay(chunk):
        at = pl.multiple_of(chunk * seg, LANES)
        slab = fac_ref[:, pl.ds(pl.multiple_of(chunk * seg, LANES), seg + LANES)]
        spread = jnp.broadcast_to(slab, (LANES, seg + LANES))
        skew = pltpu.roll(spread, 0, 1, stride=1, stride_axis=0)[:, LANES:].astype(jnp.bfloat16)
        strip[:LANES, pl.ds(at, seg)] = skew
        strip[LANES:, pl.ds(at + LANES, seg)] = skew

    def convolve(q):
        def part(w, carry):
            cols = pl.ds(pl.multiple_of(w * WIDE, LANES), WIDE)
            total = acc[:, cols]
            for k in range(seg // DEPTH):
                lag = pair * level - seg * q - DEPTH * k
                taps = strip[:, pl.ds(pl.multiple_of(lag + w * WIDE, LANES), WIDE)]
                total += jnp.dot(
                    held[q, :, k * DEPTH : (k + 1) * DEPTH], taps, preferred_element_type=jnp.float32
                )
            acc[:, cols] = total
            return carry

        lax.fori_loop(0, pair // WIDE, part, 0)

    first = 2 * (level - 1) + side
    acc[...] = jnp.zeros_like(acc)
    swap.wait_recv()
    raise_(mate)

    @pl.when(level > 0)
    def _():
        lift(first).wait_recv()
        raise_(first)

    lay(0)
    lay(1)
    conv_ref[...] = jnp.dot(noise_ref[:, :DEPTH], strip[:, :seg], preferred_element_type=jnp.float32)
    for k in range(1, seg // DEPTH):
        conv_ref[:, k * DEPTH :] += jnp.dot(
            noise_ref[:, k * DEPTH : (k + 1) * DEPTH], strip[:, : seg - k * DEPTH], preferred_element_type=jnp.float32
        )

    @pl.when(side == 1)
    def _():
        rest.wait_recv()
        for where, block in ((theirs, near), (mine, held.at[mate])):
            total = conv_ref[where]
            for k in range(seg // DEPTH):
                taps = strip[:, seg - k * DEPTH : 2 * seg - k * DEPTH]
                total += jnp.dot(block[:, k * DEPTH : (k + 1) * DEPTH], taps, preferred_element_type=jnp.float32)
            conv_ref[where] = total

    def step(j, carry):
        lay(2 * j)
        lay(2 * j + 1)
        for q in (2 * (level - j) + side, 2 * (level - j) + 1 - side):

            @pl.when(q != first)
            def _():
                lift(q).wait_recv()
                raise_(q)

            convolve(q)
        return carry

    lax.fori_loop(1, level + 1, step, 0)

    gain = column(scale_ref[...])
    gains[...] = jnp.broadcast_to(gain, gains.shape)
    back = remote(give, got, pair_send.at[1], pair_recv.at[1], {"tm": mate})

    @pl.when(level > 0)
    def _():
        give[...] = acc[:, pl.ds(pl.multiple_of((1 - side) * seg, LANES), seg)].astype(jnp.bfloat16)
        back.start()
        conv_ref[mine] = (conv_ref[mine] + acc[:, pl.ds(pl.multiple_of(side * seg, LANES), seg)]) * gains[mine, 0:1]

    @pl.when(level == 0)
    def _():
        conv_ref[...] = conv_ref[...] * gains[:, 0:1]

    for i in range(1, n):
        heard(i).wait_recv()
    before = jnp.zeros(sums.shape[1:], jnp.float32)
    for q in range(n):
        before += jnp.where(q < me, sums[q], 0.0)
    carry = column(before[0:1, :rows])
    ones = (
        lax.broadcasted_iota(jnp.int32, (DEPTH, DEPTH), 0) <= lax.broadcasted_iota(jnp.int32, (DEPTH, DEPTH), 1)
    ).astype(jnp.float32).astype(jnp.bfloat16)
    for k in range(seg // DEPTH):
        cols = slice(k * DEPTH, (k + 1) * DEPTH)
        run = jnp.dot(incb[:, cols], ones, preferred_element_type=jnp.float32) + carry
        counts_ref[:, cols] = run.astype(jnp.int32)
        steps[cell, :, cols] = jnp.broadcast_to(jnp.sum(run, axis=0, keepdims=True).astype(jnp.int32), (8, DEPTH))
        carry = run[:, DEPTH - 1 :]

    def show(i):
        return remote(steps.at[cell], steps.at[cell], step_send.at[i], step_recv.at[cell], {"cell": lax.rem(cell + i, m)})

    def seen(i):
        other = lax.rem(cell + i, m)
        return remote(steps.at[other], steps.at[other], step_send.at[i], step_recv.at[other], {"cell": other})

    for i in range(1, m):
        show(i).start()

    for i in range(1, m):
        seen(i).wait_recv()
    all_steps = steps[0, 0:1]
    for c in range(1, m):
        all_steps += steps[c, 0:1]
    total_ref[...] = all_steps

    @pl.when(level > 0)
    def _():
        back.wait_recv()
        conv_ref[theirs] = (conv_ref[theirs] + got[...].astype(jnp.float32)) * gains[theirs, 0:1]
        back.wait_send()

    @pl.when(side == 0)
    def _():
        rest.wait_send()

    swap.wait_send()
    for i in range(1, n):
        tell(i).wait_send()
    for i in range(1, m):
        show(i).wait_send()

    @pl.when(level < levels - 1)
    def _():
        def left(q, carry):
            lift(q).wait_send()
            return carry

        lax.fori_loop(0, 2 * level + 2, left, 0)


def solution(mesh):
    n, m = mesh.shape["tm"], mesh.shape["cell"]

    def shards(increments, noise, noise_scale, factor):
        rows, seg = noise.shape
        half = rows // 2
        wide = -(-rows // LANES) * LANES
        fac = jnp.pad(factor.astype(jnp.float32), (LANES, 0))[None, :]
        hbm = pl.BlockSpec(memory_space=pltpu.HBM)
        gain = noise_scale[None, :]
        vmem = pl.BlockSpec(memory_space=pltpu.VMEM)
        dma = pltpu.SemaphoreType.DMA
        counts, conv, total = pl.pallas_call(
            functools.partial(kernel, n, m),
            out_shape=(
                jax.ShapeDtypeStruct((rows, seg), jnp.int32),
                jax.ShapeDtypeStruct((rows, seg), jnp.float32),
                jax.ShapeDtypeStruct((1, seg), jnp.int32),
            ),
            in_specs=[hbm, hbm, vmem, vmem],
            out_specs=(vmem,) * 3,
            scratch_shapes=[
                pltpu.VMEM((rows, seg), jnp.int32),
                pltpu.VMEM((rows, seg), jnp.bfloat16),
                dma((2,)),
                pltpu.VMEM((n, half, seg), jnp.bfloat16),
                pltpu.VMEM((half, seg), jnp.bfloat16),
                pltpu.VMEM((DEPTH, n * seg + LANES), jnp.bfloat16),
                pltpu.VMEM((half, 2 * seg), jnp.float32),
                pltpu.VMEM((half, seg), jnp.bfloat16),
                pltpu.VMEM((half, seg), jnp.bfloat16),
                pltpu.VMEM((n, 8, wide), jnp.float32),
                pltpu.VMEM((m, 8, seg), jnp.int32),
                pltpu.VMEM((rows, seg), jnp.bfloat16),
                pltpu.VMEM((rows, LANES), jnp.float32),
                dma((n,)), dma((n,)), dma((3,)), dma((3,)), dma((n,)), dma((n,)), dma((m,)), dma((m,)),
            ],
            compiler_params=pltpu.CompilerParams(
                collective_id=0, has_side_effects=True, vmem_limit_bytes=52 * 2**20
            ),
        )(increments, noise, gain, fac)
        return counts, conv, total[0]

    return jax.shard_map(
        shards,
        mesh=mesh,
        in_specs=(P("cell", "tm"), P("cell", "tm"), P("cell"), P()),
        out_specs=(P("cell", "tm"), P("cell", "tm"), P("tm")),
        check_vma=False,
    )
```
